32 devices in a mesh: tile: 2 (over core), epoch: 16 (over z, y, x).
Axes of the slice: x: 2, y: 2, z: 4, core: 2. Of those that a mesh axis runs over, the one named last changes fastest.
Arguments:
- template: float32 [2, 256, 128], P('tile', 'epoch')
- science: bfloat16 [2, 128, 256, 128], P('tile', 'epoch')
- weights: float32 [2, 128, 256, 128], P('tile', 'epoch'), may hold values from 0.03 to 6.4
- shifts: int32 [128, 2], P('epoch'), may hold values from -8 to 8
- valid: int32 [2, 128], P('tile', 'epoch'), may hold values 0 or 1
- counts: int32 [2], P('tile'), may hold values from 32 to 128, as said below
Outputs:
- coadd: float32 [2, 256, 128], P('tile', 'epoch')
- coefficients: float32 [2, 128, 45], P('tile', 'epoch')
The draws below stay inside these ranges and needn't reach their ends.
Inputs may be any that keep to these rules, and one draw needn't show every extreme that they name: `counts`: some tile has all 128 epochs observed; epochs at or after a tile's count are unused.
All inputs are finite; a program needn't handle non-finite values. No bound on the sum of `valid` on one device may be relied on, other than what follows from the above.
Results may differ from the reference program's by a relative error of at most 0.0025.
Values may be sent and summed in bfloat16 or wider, within the bound.
A program may use at most 128 MiB of HBM per device.

```python
import jax
import jax.numpy as jnp
from jax import lax

NB = 45
HALF = 11
SHIFT = 8
W = 128
H = 256
EPOCHS = 128
TILES = 2


def spread_blocks(values):
    return jnp.broadcast_to(values, (TILES, 4, H // 4, 4, W // 4)).reshape(TILES, H, W)


def sky_field(key):
    base = jax.random.normal(key, (TILES, H, W), jnp.float32)
    row_key = jax.random.fold_in(key, 8)
    row_like = jax.random.normal(row_key, (TILES, H, 4, 1), jnp.float32)
    row_like = jnp.broadcast_to(row_like, (TILES, H, 4, W // 4)).reshape(TILES, H, W)
    col_key = jax.random.fold_in(key, 9)
    col_like = jax.random.normal(col_key, (TILES, 4, 1, W), jnp.float32)
    col_like = jnp.broadcast_to(col_like, (TILES, 4, H // 4, W)).reshape(TILES, H, W)
    mix_key = jax.random.fold_in(key, 10)
    mixes = jax.random.uniform(mix_key, (3, TILES, 4, 1, 4, 1), jnp.float32, 0.0, 1.0)
    amp_key = jax.random.fold_in(key, 5)
    amps = jnp.exp(jax.random.uniform(amp_key, (TILES, 4, 1, 4, 1), jnp.float32, -0.8, 0.8))
    rough = spread_blocks(0.3 + 0.7 * mixes[0]) * base
    streaks = spread_blocks(1.2 * mixes[1]) * row_like + spread_blocks(1.2 * mixes[2]) * col_like
    return spread_blocks(amps) * (rough + streaks)


def draw_template(key, part):
    sky = sky_field(key)
    key = jax.random.fold_in(key, 11)
    rows = jnp.arange(H).astype(jnp.float32)
    ramp = (0.5 + rows / H)[None, :, None]
    return sky + ramp + 0.3 * jax.random.normal(key, (TILES, H, W), jnp.float32)


def draw_science(key, part):
    sky = sky_field(key)
    key = jax.random.fold_in(key, 12)
    amp_key, noise_key = jax.random.split(key)
    amp = jnp.exp(jax.random.uniform(amp_key, (TILES, EPOCHS, 1, 1), jnp.float32, -0.69, 0.69))
    noise = jax.random.normal(noise_key, (TILES, EPOCHS, H, W), jnp.float32)
    return (amp * sky[:, None] + 0.8 * noise).astype(jnp.bfloat16)


def draw_weights(key, part):
    key = jax.random.fold_in(key, 14)
    level_key, jitter_key, column_key = jax.random.split(key, 3)
    levels = jnp.exp(jax.random.uniform(level_key, (TILES, EPOCHS, 4, 1, 4, 1), jnp.float32, -1.5, 1.5))
    levels = jnp.broadcast_to(levels, (TILES, EPOCHS, 4, H // 4, 4, W // 4)).reshape(TILES, EPOCHS, H, W)
    jitter = jnp.exp(jax.random.uniform(jitter_key, (TILES, EPOCHS, H, W), jnp.float32, -0.35, 0.35))
    flagged = jax.random.randint(column_key, (TILES, EPOCHS, 1, W), 0, 32) == 0
    damping = jnp.where(flagged, 0.2, 1.0).astype(jnp.float32)
    return levels * jitter * damping


def draw_counts(key, part):
    key = jax.random.fold_in(key, 13)
    first, second = jax.random.split(key)
    drawn = jax.random.randint(first, (TILES,), EPOCHS // 4, EPOCHS + 1)
    chosen = jax.random.randint(second, (), 0, TILES)
    return jnp.where(jnp.arange(TILES) == chosen, EPOCHS, drawn).astype(jnp.int32)


def plant(values, own_key, low, largest):
    longest = values.shape.index(max(values.shape))
    spots = []
    for shift in (0, 1):
        where = [jax.random.randint(jax.random.fold_in(own_key, axis), (), 0, length) for axis, length in enumerate(values.shape)]
        where[longest] = (where[longest] + shift) % values.shape[longest]
        spots.append(tuple(where))
    return values.at[spots[0]].set(low).at[spots[1]].set(largest)


def setup_inputs(seed: int = 0) -> dict:
    splits = jax.random.split(jax.random.key(seed), 7)
    return {
        "template": draw_template(jax.random.fold_in(splits[6], 71), 0),
        "science": draw_science(jax.random.fold_in(splits[6], 71), 0),
        "weights": draw_weights(jax.random.fold_in(splits[6], 71), 0),
        "shifts": plant(jax.random.randint(splits[3], (EPOCHS, 2), 0 - SHIFT, SHIFT + 1), jax.random.fold_in(splits[3], 1), 0 - SHIFT, SHIFT).astype(jnp.int32),
        "valid": plant((jax.random.randint(splits[4], (TILES, EPOCHS), 0, 5) < 4).astype(jnp.int32), jax.random.fold_in(splits[4], 1), 0, 1),
        "counts": draw_counts(jax.random.fold_in(splits[6], 71), 0),
    }


SIGMAS = (0.75, 1.5, 3.0)
RIDGE = 0.5

def profile(offset, sigma, power):
    ratio = offset / sigma
    values = ratio ** power * jnp.exp(-0.5 * ratio * ratio)
    return jnp.where(jnp.abs(offset) <= HALF, values, 0.0)

def row_filter(width, sigma, power):
    inner = lax.broadcasted_iota(jnp.int32, (width + 2 * HALF, width), 0)
    outer = lax.broadcasted_iota(jnp.int32, (width + 2 * HALF, width), 1)
    return profile((outer + HALF - inner).astype(jnp.float32), sigma, power)

def col_filter(start, rows, height, sigma, power):
    outer = lax.broadcasted_iota(jnp.int32, (rows, height), 0) + start
    inner = lax.broadcasted_iota(jnp.int32, (rows, height), 1)
    return profile((outer - inner).astype(jnp.float32), sigma, power)

def basis_images(padded, start, rows):
    pieces = []
    for sigma in SIGMAS:
        for power in range(5):
            filtered = jnp.dot(padded, row_filter(W, sigma, power), precision=lax.Precision.HIGHEST)
            for second in range(5 - power):
                band = col_filter(start, rows, H, sigma, second)
                pieces.append(jnp.dot(band, filtered, precision=lax.Precision.HIGHEST).astype(jnp.bfloat16))
    return jnp.stack(pieces)

def fit_epoch(basis, image, weight):
    weighted = (basis * weight).astype(jnp.bfloat16)
    gram = lax.dot_general(weighted.astype(jnp.float32), basis.astype(jnp.float32), (((1,), (1,)), ((), ())), preferred_element_type=jnp.float32)
    gram = 0.5 * (gram + gram.T)
    proj = jnp.dot(weighted.astype(jnp.float32), image.astype(jnp.float32), preferred_element_type=jnp.float32)
    scale = jnp.sqrt(jnp.diagonal(gram) + 1e-06)
    system = gram / (scale[:, None] * scale[None, :]) + RIDGE * jnp.eye(NB, dtype=jnp.float32)
    factor = jnp.linalg.cholesky(system)
    first = lax.linalg.triangular_solve(factor, (proj / scale)[:, None], left_side=True, lower=True)
    coef = lax.linalg.triangular_solve(factor, first, left_side=True, lower=True, transpose_a=True)[:, 0]
    model = jnp.dot((coef / scale).astype(jnp.bfloat16).astype(jnp.float32), basis.astype(jnp.float32), preferred_element_type=jnp.float32)
    return (coef, image.astype(jnp.float32) - model)

def warp(field, rise, run, width):
    rows = jnp.pad(field, ((SHIFT, SHIFT), (0, 0)))
    return lax.dynamic_slice(rows, (SHIFT - rise, SHIFT - run), (H, width))

def reference(template, science, weights, shifts, valid, counts):
    centred = template - lax.optimization_barrier(jnp.mean(template, axis=(1, 2), keepdims=True))
    full = jnp.concatenate([centred[t] for t in range(TILES)], axis=1)
    padded = jnp.pad(full, ((0, 0), (HALF, HALF)))
    bases = [basis_images(padded[:, t * W:t * W + W + 2 * HALF], 0, H).reshape(NB, H * W) for t in range(TILES)]
    order = jnp.arange(EPOCHS).astype(jnp.int32)
    live_all = (valid * (order[None, :] < counts[:, None]).astype(jnp.int32)).astype(jnp.float32)

    def step(carry, epoch):
        numer, total = carry
        coefs = []
        prods = []
        masses = []
        for t in range(TILES):
            live = live_all[t, epoch]
            weight = weights[t, epoch]
            coef, diff = fit_epoch(bases[t], science[t, epoch].reshape(H * W), weight.reshape(H * W))
            coefs.append(live * coef)
            prods.append(live * weight * diff.reshape(H, W))
            masses.append(live * weight)
        prod_full = jnp.pad(jnp.concatenate(prods, axis=1), ((0, 0), (SHIFT, SHIFT)))
        mass_full = jnp.pad(jnp.concatenate(masses, axis=1), ((0, 0), (SHIFT, SHIFT)))
        rise = shifts[epoch, 0]
        run = shifts[epoch, 1]
        numer = numer + warp(prod_full, rise, run, TILES * W)
        total = total + warp(mass_full, rise, run, TILES * W)
        return ((numer, total), jnp.stack(coefs))
    start = (jnp.zeros((H, TILES * W), jnp.float32), jnp.zeros((H, TILES * W), jnp.float32))
    (numer, total), coefs = lax.scan(step, start, order)
    coadd_full = numer / jnp.sqrt(1.0 + total)
    coadd = jnp.transpose(coadd_full.reshape(H, TILES, W), (1, 0, 2))
    return (coadd, jnp.transpose(coefs, (1, 0, 2)))
```

```python
import functools

import jax
import jax.numpy as jnp
import ml_dtypes
import numpy as np
from jax import lax
from jax.experimental import pallas as pl
from jax.experimental.pallas import tpu as pltpu
from jax.sharding import PartitionSpec as P

NB = 45
NBP = 48
HALF = 11
SHIFT = 8
W = 128
H = 256
G = 16
WIN = 3 * G
SIGMAS = (0.75, 1.5, 3.0)
NF = 15
RIDGE = 0.5
SCI = 16
MESH = pl.DeviceIdType.MESH
VMEM = pl.BlockSpec(memory_space=pltpu.VMEM)
SMEM = pl.BlockSpec(memory_space=pltpu.SMEM)


def taps(offset, sigma, power):
    ratio = offset.astype(np.float64) / sigma
    values = ratio**power * np.exp(-0.5 * ratio * ratio)
    return np.where(np.abs(offset) <= HALF, values, 0.0)


def split(values):
    values = values.astype(np.float32)
    high = values.astype(ml_dtypes.bfloat16)
    low = (values - high.astype(np.float32)).astype(ml_dtypes.bfloat16)
    return high, low


def column_taps():
    spot = np.arange(W)
    source = np.concatenate([spot, np.where(spot < W // 2, spot + W, spot - W)])
    offset = spot[None, :] - source[:, None]
    return split(np.concatenate([taps(offset, s, p) for s in SIGMAS for p in range(5)], axis=1))


def row_taps():
    offset = np.arange(G)[:, None] + G - np.arange(WIN)[None, :]
    out = np.zeros((G, NBP, NF, WIN))
    b = 0
    for i, sigma in enumerate(SIGMAS):
        for p in range(5):
            for q in range(5 - p):
                out[:, b, i * 5 + p, :] = taps(offset, sigma, q)
                b += 1
    return split(out.reshape(G * NBP, NF * WIN))


def spreads(epochs):
    tile = np.zeros((NBP, G, NBP))
    tile[np.arange(NBP), :, np.arange(NBP)] = 1.0
    keep = np.zeros((epochs, G, G, NBP))
    keep[:, np.arange(G), np.arange(G), :] = 1.0
    return (
        tile.reshape(NBP, G * NBP).astype(ml_dtypes.bfloat16),
        keep.reshape(epochs * G, G * NBP).astype(np.float32),
    )


def greet(tiles, epochs, tile, me):
    barrier = pltpu.get_barrier_semaphore()

    def hello(step, carry):
        peer = lax.rem(me + step, epochs)
        pl.semaphore_signal(barrier, inc=1, device_id=(tile, peer), device_id_type=MESH)
        return carry

    lax.fori_loop(1, epochs, hello, 0)
    for step in (1, tiles - 1):
        near = lax.rem(tile + step, tiles)
        pl.semaphore_signal(barrier, inc=1, device_id=(near, me), device_id_type=MESH)
    pl.semaphore_wait(barrier, epochs + 1)


def gather_kernel(tiles, epochs, rows, mine, own, left, right, send, recv, side_send, side_recv, local):
    tile = lax.axis_index("tile")
    me = lax.axis_index("epoch")
    greet(tiles, epochs, tile, me)

    def band(which):
        return pl.ds(pl.multiple_of(which * rows, rows), rows)

    def copy(step):
        peer = lax.rem(me + step, epochs)
        return pltpu.make_async_remote_copy(
            src_ref=mine,
            dst_ref=own.at[band(me)],
            send_sem=send.at[step],
            recv_sem=recv.at[step],
            device_id=(tile, peer),
            device_id_type=MESH,
        )

    def start(step, carry):
        copy(step).start()
        return carry

    def finish(step, carry):
        copy(step).wait_recv()
        copy(step).wait_send()
        return carry

    lax.fori_loop(1, epochs, start, 0)
    here = pltpu.make_async_copy(mine, own.at[band(me)], local)
    here.start()
    here.wait()
    lax.fori_loop(1, epochs, finish, 0)
    sides = []
    for i, (step, target) in enumerate(((1, left), (tiles - 1, right))):
        side = pltpu.make_async_remote_copy(
            src_ref=own,
            dst_ref=target,
            send_sem=side_send.at[i],
            recv_sem=side_recv.at[i],
            device_id=(lax.rem(tile + step, tiles), me),
            device_id_type=MESH,
        )
        side.start()
        sides.append(side)
    for side in sides:
        side.wait()


def gather(mesh_sizes, template):
    tiles, epochs = mesh_sizes
    rows = template.shape[0]
    whole = jax.ShapeDtypeStruct((H, W), jnp.float32)
    return pl.pallas_call(
        functools.partial(gather_kernel, tiles, epochs, rows),
        out_shape=(whole, whole, whole),
        in_specs=[VMEM],
        out_specs=(VMEM, VMEM, VMEM),
        scratch_shapes=[
            pltpu.SemaphoreType.DMA((epochs,)),
            pltpu.SemaphoreType.DMA((epochs,)),
            pltpu.SemaphoreType.DMA((2,)),
            pltpu.SemaphoreType.DMA((2,)),
            pltpu.SemaphoreType.DMA,
        ],
        compiler_params=pltpu.CompilerParams(collective_id=0, has_side_effects=True),
        name="gather_template",
    )(template)


def dot(a, b):
    return jnp.dot(a, b, preferred_element_type=jnp.float32)


def halves(values):
    high = values.astype(jnp.bfloat16)
    return high, (values - high.astype(jnp.float32)).astype(jnp.bfloat16)


def fit_kernel(
    tiles, epochs,
    own, left, right, turned, science, weights, shifts, valid, counts, ch, cl, rh, rl, spread, keep,
    coef_out, sky_out, spill_out,
    fh, fl, basis, lhs, rhs, gram, moved,
):
    tile = lax.axis_index("tile")
    me = lax.axis_index("epoch")
    here = science.shape[0]

    mean = 1.0 / (H * W)
    lane = lax.broadcasted_iota(jnp.int32, (H, W), 1)
    mid = own[...] - jnp.sum(own[...]) * mean
    before = (left[...] - jnp.sum(left[...]) * mean) * (tile > 0).astype(jnp.float32)
    after = (right[...] - jnp.sum(right[...]) * mean) * (tile < tiles - 1).astype(jnp.float32)
    ref = jnp.concatenate([mid, jnp.where(lane < W // 2, after, before)], axis=1)
    high, low = halves(ref)
    zeros = jnp.zeros((NF, G, W), jnp.bfloat16)
    for buf in (fh, fl):
        buf[:, 0:G, :] = zeros
        buf[:, G + H : G + H + G, :] = zeros
    for f in range(NF):
        cols = slice(f * W, (f + 1) * W)
        out = dot(high, ch[:, cols]) + (dot(low, ch[:, cols]) + dot(high, cl[:, cols]))
        fhigh, flow = halves(out)
        fh[f, G : G + H, :] = fhigh
        fl[f, G : G + H, :] = flow

    gram[...] = jnp.zeros_like(gram)

    def block(i, carry):
        top = pl.multiple_of(i * G, G)
        wh = fh[:, pl.ds(top, WIN), :].reshape(NF * WIN, W)
        wl = fl[:, pl.ds(top, WIN), :].reshape(NF * WIN, W)
        both = dot(rh[...], jnp.concatenate([wh, wl], axis=1))
        values = both[:, :W] + (both[:, W:] + dot(rl[...], wh))
        values = values.astype(jnp.bfloat16)
        basis[pl.ds(pl.multiple_of(i * (G * NBP), G * NBP), G * NBP), :] = values
        for r in range(G):
            cols = slice(r * W, (r + 1) * W)
            part = values[r * NBP : (r + 1) * NBP, :]
            rhs[0:NBP, cols] = part
            rhs[NBP : NBP + SCI, cols] = turned[top + r]
            wide = part.astype(jnp.float32)
            for e in range(here):
                lhs[e * NBP : (e + 1) * NBP, cols] = (
                    wide * weights[e, pl.ds(top + r, 1), :]
                ).astype(jnp.bfloat16)
        gram[...] += lax.dot_general(
            lhs[...], rhs[...], (((1,), (1,)), ((), ())), preferred_element_type=jnp.float32
        )
        return carry

    lax.fori_loop(0, H // G, block, 0)

    wide = NBP + SCI
    eye = (
        lax.broadcasted_iota(jnp.int32, (NBP, NBP), 0)
        == lax.broadcasted_iota(jnp.int32, (NBP, NBP), 1)
    ).astype(jnp.float32)
    col = lax.broadcasted_iota(jnp.int32, (NBP, SCI), 1)
    systems = []
    scales = []
    for e in range(here):
        full = gram[e * NBP : (e + 1) * NBP, :]
        square = full[:, :NBP]
        square = 0.5 * (square + square.T)
        diag = square * eye
        down = lax.rsqrt(jnp.sum(diag, axis=1, keepdims=True) + 1e-06)
        across = lax.rsqrt(jnp.sum(diag, axis=0, keepdims=True) + 1e-06)
        proj = jnp.sum(jnp.where(col == e, full[:, NBP:], 0.0), axis=1, keepdims=True) * down
        square = square * (down * across) + RIDGE * eye
        systems.append(jnp.concatenate([square, jnp.where(col == 0, proj, 0.0)], axis=1))
        scales.append(across)
    a = jnp.stack(systems)
    row = lax.broadcasted_iota(jnp.int32, (here, NBP, 1), 1)
    for k in range(NB):
        pivot = a[:, k : k + 1, :]
        pivot = pivot * (1.0 / pivot[:, :, k : k + 1])
        factor = jnp.where(row == k, 0.0, a[:, :, k : k + 1])
        a = a - factor * pivot
    ys = []
    for e in range(here):
        diag = jnp.sum(a[e, :, :NBP] * eye, axis=1, keepdims=True)
        ys.append(jnp.sum((a[e, :, NBP : NBP + 1] / diag) * eye, axis=0, keepdims=True))
    lives = [
        (valid[0, e] * (me * here + e < counts[0]).astype(jnp.int32)).astype(jnp.float32)
        for e in range(here)
    ]
    coef_out[...] = jnp.concatenate([lives[e] * ys[e] for e in range(here)], axis=0)[:, :NB]
    ks = jnp.concatenate([ys[e] * scales[e] for e in range(here)], axis=0).astype(jnp.bfloat16)
    spun = dot(ks, spread[...])
    spun = jnp.broadcast_to(spun[:, None, :], (here, G, G * NBP)).reshape(here * G, G * NBP)
    mixer = (spun * keep[...]).astype(jnp.bfloat16)

    moved[:, :, 0:SHIFT, :] = jnp.zeros((here, 2, SHIFT, W), jnp.float32)
    moved[:, :, SHIFT + H :, :] = jnp.zeros((here, 2, SHIFT, W), jnp.float32)

    def differ(i, carry):
        top = pl.multiple_of(i * G, G)
        part = basis[pl.ds(pl.multiple_of(i * (G * NBP), G * NBP), G * NBP), :]
        model = dot(mixer, part)
        for e in range(here):
            diff = science[e, pl.ds(top, G), :].astype(jnp.float32) - model[e * G : (e + 1) * G, :]
            mass = lives[e] * weights[e, pl.ds(top, G), :]
            run = lax.rem(shifts[e, 1] + W, W)
            spot = pl.ds(pl.multiple_of(top + SHIFT, SHIFT), G)
            moved[e, 0, spot, :] = pltpu.roll(mass * diff, run, 1)
            moved[e, 1, spot, :] = pltpu.roll(mass, run, 1)
        return carry

    lax.fori_loop(0, H // G, differ, 0)

    bands, _, rows, _ = sky_out.shape
    for field in range(2):
        sky = jnp.zeros((H, W), jnp.float32)
        spill = jnp.zeros((H, W), jnp.float32)
        for e in range(here):
            values = moved[e, field, pl.ds(SHIFT - shifts[e, 0], H), :]
            source = lane - shifts[e, 1]
            inside = (source >= 0) & (source < W)
            sky += jnp.where(inside, values, 0.0)
            spill += jnp.where(inside, 0.0, values)
        sky_out[:, field] = sky.reshape(bands, rows, W)
        spill_out[:, field] = spill.reshape(bands, rows, W)


def fit(mesh_sizes, rows, own, left, right, turned, science, weights, shifts, valid, counts):
    tiles, epochs = mesh_sizes
    here = science.shape[0]
    ch, cl = column_taps()
    rh, rl = row_taps()
    spread, keep = spreads(here)
    sky = jax.ShapeDtypeStruct((epochs, 2, rows, W), jnp.float32)
    return pl.pallas_call(
        functools.partial(fit_kernel, tiles, epochs),
        out_shape=(jax.ShapeDtypeStruct((here, NB), jnp.float32), sky, sky),
        in_specs=[VMEM] * 6 + [SMEM] * 3 + [VMEM] * 6,
        out_specs=(VMEM, VMEM, VMEM),
        scratch_shapes=[
            pltpu.VMEM((NF, H + 2 * G, W), jnp.bfloat16),
            pltpu.VMEM((NF, H + 2 * G, W), jnp.bfloat16),
            pltpu.VMEM((H * NBP, W), jnp.bfloat16),
            pltpu.VMEM((here * NBP, G * W), jnp.bfloat16),
            pltpu.VMEM((NBP + SCI, G * W), jnp.bfloat16),
            pltpu.VMEM((here * NBP, NBP + SCI), jnp.float32),
            pltpu.VMEM((here, 2, H + 2 * SHIFT, W), jnp.float32),
        ],
        compiler_params=pltpu.CompilerParams(vmem_limit_bytes=48 * 1024 * 1024),
        name="fit_epochs",
    )(own, left, right, turned, science, weights, shifts, valid, counts, ch, cl, rh, rl, spread, keep)


def coadd_kernel(
    tiles, epochs, sky, spill, out, whole, from_left, from_right, parts, send, recv, side_send, side_recv
):
    tile = lax.axis_index("tile")
    me = lax.axis_index("epoch")
    greet(tiles, epochs, tile, me)
    sides = []
    for i, (step, target) in enumerate(((1, from_left), (tiles - 1, from_right))):
        side = pltpu.make_async_remote_copy(
            src_ref=spill,
            dst_ref=target,
            send_sem=side_send.at[i],
            recv_sem=side_recv.at[i],
            device_id=(lax.rem(tile + step, tiles), me),
            device_id_type=MESH,
        )
        side.start()
        sides.append(side)
    for side in sides:
        side.wait()
    lane = lax.broadcasted_iota(jnp.int32, sky.shape, 3)
    has_left = (tile > 0).astype(jnp.float32)
    has_right = (tile < tiles - 1).astype(jnp.float32)
    whole[...] = sky[...] + (
        jnp.where(lane < SHIFT, from_left[...], 0.0) * has_left
        + jnp.where(lane >= W - SHIFT, from_right[...], 0.0) * has_right
    )

    def copy(step):
        peer = lax.rem(me + step, epochs)
        return pltpu.make_async_remote_copy(
            src_ref=whole.at[peer],
            dst_ref=parts.at[step],
            send_sem=send.at[step],
            recv_sem=recv.at[step],
            device_id=(tile, peer),
            device_id_type=MESH,
        )

    def start(step, carry):
        copy(step).start()
        return carry

    def finish(step, total):
        copy(step).wait_recv()
        copy(step).wait_send()
        return total + parts[step]

    lax.fori_loop(1, epochs, start, 0)
    total = lax.fori_loop(1, epochs, finish, whole[me])
    out[...] = total[0] / jnp.sqrt(1.0 + total[1])


def coadd(mesh_sizes, sky, spill):
    tiles, epochs = mesh_sizes
    rows = sky.shape[2]
    return pl.pallas_call(
        functools.partial(coadd_kernel, tiles, epochs),
        out_shape=jax.ShapeDtypeStruct((rows, W), jnp.float32),
        in_specs=[VMEM, VMEM],
        out_specs=VMEM,
        scratch_shapes=[
            pltpu.VMEM(sky.shape, jnp.float32),
            pltpu.VMEM(sky.shape, jnp.float32),
            pltpu.VMEM(sky.shape, jnp.float32),
            pltpu.VMEM(sky.shape, jnp.float32),
            pltpu.SemaphoreType.DMA((epochs,)),
            pltpu.SemaphoreType.DMA((epochs,)),
            pltpu.SemaphoreType.DMA((2,)),
            pltpu.SemaphoreType.DMA((2,)),
        ],
        compiler_params=pltpu.CompilerParams(collective_id=1, has_side_effects=True),
        name="coadd_bands",
    )(sky, spill)


def local(mesh_sizes, template, science, weights, shifts, valid, counts):
    here = science.shape[1]
    turned = jnp.transpose(science[0], (1, 0, 2))
    turned = jnp.pad(turned, ((0, 0), (0, SCI - here), (0, 0)))
    own, left, right = gather(mesh_sizes, template[0])
    coefs, sky, spill = fit(
        mesh_sizes, template.shape[1], own, left, right, turned, science[0], weights[0], shifts, valid, counts
    )
    return (coadd(mesh_sizes, sky, spill)[None], coefs[None])


def solution(mesh):
    sizes = (mesh.shape["tile"], mesh.shape["epoch"])
    in_specs = (
        P("tile", "epoch", None),
        P("tile", "epoch", None, None),
        P("tile", "epoch", None, None),
        P("epoch", None),
        P("tile", "epoch"),
        P("tile"),
    )
    out_specs = (P("tile", "epoch", None), P("tile", "epoch", None))
    return jax.shard_map(
        functools.partial(local, sizes), mesh=mesh, in_specs=in_specs, out_specs=out_specs, check_vma=False
    )
```

```python
import functools

import jax
import jax.numpy as jnp
import numpy as np
from jax import lax
from jax.experimental import pallas as pl
from jax.experimental.pallas import tpu as pltpu
from jax.sharding import PartitionSpec as P

NB = 45
PER = 16
HALF = 11
SHIFT = 8
W = 128
H = 256
G = 16
WIN = 3 * G
SIGMAS = (0.75, 1.5, 3.0)
NF = 15
NS = 3
NBP = NS * PER
RIDGE = 0.5
SCI = 16
MESH = pl.DeviceIdType.MESH
VMEM = pl.BlockSpec(memory_space=pltpu.VMEM)
SMEM = pl.BlockSpec(memory_space=pltpu.SMEM)
HBM = pl.BlockSpec(memory_space=pltpu.HBM)


def taps(offset, sigma, power):
    ratio = offset.astype(np.float64) / sigma
    values = ratio**power * np.exp(-0.5 * ratio * ratio)
    return np.where(np.abs(offset) <= HALF, values, 0.0)


def column_taps():
    spot = np.arange(W)
    source = np.concatenate([spot, np.where(spot < W // 2, spot + W, spot - W)])
    offset = spot[None, :] - source[:, None]
    return np.concatenate([taps(offset, s, p) for s in SIGMAS for p in range(5)], axis=1).astype(np.float32)


def row_taps():
    offset = np.arange(G)[:, None] + G - np.arange(WIN)[None, :]
    out = np.zeros((NS, G, PER, 5, WIN))
    for i, sigma in enumerate(SIGMAS):
        for b, (p, q) in enumerate((p, q) for p in range(5) for q in range(5 - p)):
            out[i, :, b, p, :] = taps(offset, sigma, q)
    return out.reshape(NS, G * PER, 5 * WIN).astype(np.float32)


def greet(tiles, epochs, tile, me):
    barrier = pltpu.get_barrier_semaphore()

    def hello(step, carry):
        peer = lax.rem(me + step, epochs)
        pl.semaphore_signal(barrier, inc=1, device_id=(tile, peer), device_id_type=MESH)
        return carry

    lax.fori_loop(1, epochs, hello, 0)
    for step in (1, tiles - 1):
        near = lax.rem(tile + step, tiles)
        pl.semaphore_signal(barrier, inc=1, device_id=(near, me), device_id_type=MESH)
    pl.semaphore_wait(barrier, epochs + 1)


def dot(a, b):
    return jnp.dot(a, b, preferred_element_type=jnp.float32)


def halves(values):
    high = values.astype(jnp.bfloat16)
    return high, (values - high.astype(jnp.float32)).astype(jnp.bfloat16)


def iota(shape, axis):
    return lax.broadcasted_iota(jnp.int32, shape, axis)


def kernel(
    tiles, epochs,
    template, science_hbm, weights_hbm, shifts, valid, counts, col_hbm, row_hbm,
    coadd_out, coef_out,
    science, weights, col_wide, row_wide, ch, cl, rh, rl,
    own, left, right, fh, fl, basis, lhs, rhs, gram, moved, whole, spill, from_left, from_right, parts,
    load, send, recv, side_send, side_recv,
):
    tile = lax.axis_index("tile")
    me = lax.axis_index("epoch")
    here = science.shape[0]
    bands, rows = whole.shape[1], whole.shape[2]
    lane = iota((H, W), 1)
    has_left = (tile > 0).astype(jnp.float32)
    has_right = (tile < tiles - 1).astype(jnp.float32)

    loads = [
        pltpu.make_async_copy(src, dst, load.at[i])
        for i, (src, dst) in enumerate(
            ((weights_hbm, weights), (col_hbm, col_wide), (row_hbm, row_wide), (science_hbm, science))
        )
    ]
    for one in loads:
        one.start()
    greet(tiles, epochs, tile, me)

    def to_peers(kind, source, target):
        def copy(step):
            return pltpu.make_async_remote_copy(
                src_ref=source(lax.rem(me + step, epochs)),
                dst_ref=target(step),
                send_sem=send.at[kind, step],
                recv_sem=recv.at[kind, step],
                device_id=(tile, lax.rem(me + step, epochs)),
                device_id_type=MESH,
            )

        def start(step, carry):
            copy(step).start()
            return carry

        def finish(step, carry):
            copy(step).wait_recv()
            copy(step).wait_send()
            return carry

        lax.fori_loop(1, epochs, start, 0)
        return lambda: lax.fori_loop(1, epochs, finish, 0)

    def to_sides(kind, source, to_right, to_left):
        sides = [
            pltpu.make_async_remote_copy(
                src_ref=source,
                dst_ref=target,
                send_sem=side_send.at[kind, i],
                recv_sem=side_recv.at[kind, i],
                device_id=(lax.rem(tile + step, tiles), me),
                device_id_type=MESH,
            )
            for i, (step, target) in enumerate(((1, to_right), (tiles - 1, to_left)))
        ]
        for side in sides:
            side.start()

        def finish():
            for side in sides:
                side.wait()

        return finish

    band = pl.ds(pl.multiple_of(me * rows, rows), rows)
    template_done = to_peers(0, lambda peer: template, lambda step: own.at[band])
    own[band, :] = template[...]

    lives = [
        (valid[0, e] * (me * here + e < counts[0]).astype(jnp.int32)).astype(jnp.float32)
        for e in range(here)
    ]
    runs = [lax.rem(shifts[e, 1] + W, W) for e in range(here)]

    def gather_sky(field):
        sky = jnp.zeros((H, W), jnp.float32)
        over = jnp.zeros((H, W), jnp.float32)
        for e in range(here):
            values = moved[e, pl.ds(SHIFT - shifts[e, 0], H), :]
            origin = lane - shifts[e, 1]
            inside = (origin >= 0) & (origin < W)
            sky += jnp.where(inside, values, 0.0)
            over += jnp.where(inside, 0.0, values)
        whole[field] = sky.reshape(bands, rows, W)
        spill[field] = over.reshape(bands, rows, W)
        return to_sides(1 + field, spill.at[field], from_left.at[field], from_right.at[field])

    def merge(field):
        spot = iota((bands, rows, W), 2)
        whole[field] = whole[field] + (
            jnp.where(spot < SHIFT, from_left[field], 0.0) * has_left
            + jnp.where(spot >= W - SHIFT, from_right[field], 0.0) * has_right
        )
        return to_peers(
            1 + field, lambda peer: whole.at[field, peer], lambda step: parts.at[field, step]
        )

    def total_of(field):
        def add(step, total):
            return total + parts[field, step]

        return lax.fori_loop(1, epochs, add, whole[field, me])

    moved[:, 0:SHIFT, :] = jnp.zeros((here, SHIFT, W), jnp.float32)
    moved[:, SHIFT + H :, :] = jnp.zeros((here, SHIFT, W), jnp.float32)
    loads[0].wait()
    for e in range(here):
        moved[e, SHIFT : SHIFT + H, :] = pltpu.roll(lives[e] * weights[e], runs[e], 1)
    mass_sides = gather_sky(0)

    template_done()
    tile_sides = to_sides(0, own, left, right)
    mass_sides()
    mass_done = merge(0)

    loads[1].wait()
    ch[...], cl[...] = halves(col_wide[...])
    loads[2].wait()
    rh[...], rl[...] = halves(row_wide[...])
    zeros = jnp.zeros((NF, G, W), jnp.bfloat16)
    for buf in (fh, fl):
        buf[:, 0:G, :] = zeros
        buf[:, G + H : G + H + G, :] = zeros
    gram[...] = jnp.zeros_like(gram)
    tile_sides()

    mean = 1.0 / (H * W)
    mid = own[...] - jnp.sum(own[...]) * mean
    before = (left[...] - jnp.sum(left[...]) * mean) * has_left
    after = (right[...] - jnp.sum(right[...]) * mean) * has_right
    high, low = halves(jnp.concatenate([mid, jnp.where(lane < W // 2, after, before)], axis=1))
    for f in range(NF):
        cols = slice(f * W, (f + 1) * W)
        out = dot(high, ch[:, cols]) + (dot(low, ch[:, cols]) + dot(high, cl[:, cols]))
        fhigh, flow = halves(out)
        fh[f, G : G + H, :] = fhigh
        fl[f, G : G + H, :] = flow

    loads[3].wait()
    turn_to = iota((G * SCI, here * G), 0)
    turn_from = iota((G * SCI, here * G), 1)
    turn = (
        (turn_to // SCI == turn_from % G) & (turn_to % SCI == turn_from // G)
    ).astype(jnp.float32).astype(jnp.bfloat16)

    def block(i, carry):
        top = pl.multiple_of(i * G, G)
        pieces = []
        for s in range(NS):
            wh = fh[5 * s : 5 * s + 5, pl.ds(top, WIN), :].reshape(5 * WIN, W)
            wl = fl[5 * s : 5 * s + 5, pl.ds(top, WIN), :].reshape(5 * WIN, W)
            both = dot(rh[s], jnp.concatenate([wh, wl], axis=1))
            values = both[:, :W] + (both[:, W:] + dot(rl[s], wh))
            pieces.append(values.astype(jnp.bfloat16))
            first = pl.multiple_of(i * (G * NBP) + s * (G * PER), G * PER)
            basis[pl.ds(first, G * PER), :] = pieces[s]
        images = science[:, pl.ds(top, G), :].reshape(here * G, W)
        turned = dot(turn, images).astype(jnp.bfloat16)
        for r in range(G):
            cols = slice(r * W, (r + 1) * W)
            part = jnp.concatenate([piece[r * PER : (r + 1) * PER, :] for piece in pieces], axis=0)
            rhs[0:NBP, cols] = part
            rhs[NBP : NBP + SCI, cols] = turned[r * SCI : (r + 1) * SCI, :]
            wide = part.astype(jnp.float32)
            for e in range(here):
                lhs[e * NBP : (e + 1) * NBP, cols] = (
                    wide * weights[e, pl.ds(top + r, 1), :]
                ).astype(jnp.bfloat16)
        gram[...] += lax.dot_general(
            lhs[...], rhs[...], (((1,), (1,)), ((), ())), preferred_element_type=jnp.float32
        )
        return carry

    lax.fori_loop(0, H // G, block, 0)

    eye = (iota((NBP, NBP), 0) == iota((NBP, NBP), 1)).astype(jnp.float32)
    col = iota((NBP, SCI), 1)
    systems = []
    scales = []
    for e in range(here):
        full = gram[e * NBP : (e + 1) * NBP, :]
        square = full[:, :NBP]
        square = 0.5 * (square + square.T)
        diag = square * eye
        down = lax.rsqrt(jnp.sum(diag, axis=1, keepdims=True) + 1e-06)
        across = lax.rsqrt(jnp.sum(diag, axis=0, keepdims=True) + 1e-06)
        proj = jnp.sum(jnp.where(col == e, full[:, NBP:], 0.0), axis=1, keepdims=True) * down
        square = square * (down * across) + RIDGE * eye
        systems.append(jnp.concatenate([square, jnp.where(col == 0, proj, 0.0)], axis=1))
        scales.append(across)
    a = jnp.stack(systems)
    row = iota((here, NBP, 1), 1)
    for k in range(0, NBP, 2):
        r0, r1 = a[:, k : k + 1, :], a[:, k + 1 : k + 2, :]
        c0, c1 = a[:, :, k : k + 1], a[:, :, k + 1 : k + 2]
        p00, p01 = r0[:, :, k : k + 1], r0[:, :, k + 1 : k + 2]
        p10, p11 = r1[:, :, k : k + 1], r1[:, :, k + 1 : k + 2]
        inverse = 1.0 / (p00 * p11 - p01 * p10)
        q0 = (p11 * inverse) * r0 - (p01 * inverse) * r1
        q1 = (p00 * inverse) * r1 - (p10 * inverse) * r0
        a = a - (c0 - (row == k).astype(jnp.float32)) * q0 - (c1 - (row == k + 1).astype(jnp.float32)) * q1
    ys = [jnp.sum(a[e, :, NBP : NBP + 1] * eye, axis=0, keepdims=True) for e in range(here)]
    coefs = jnp.concatenate([lives[e] * ys[e] for e in range(here)], axis=0)
    coef_out[...] = jnp.concatenate(
        [coefs[:, s * PER : (s + 1) * PER - 1] for s in range(NS)], axis=1
    )
    ks = jnp.concatenate([ys[e] * scales[e] for e in range(here)], axis=0).astype(jnp.bfloat16)
    lanes = iota((NBP, G * NBP), 1)
    spread = (lanes // (G * PER) * PER + lanes % PER == iota((NBP, G * NBP), 0)).astype(jnp.float32).astype(jnp.bfloat16)
    spun = dot(ks, spread)
    spun = jnp.broadcast_to(spun[:, None, :], (here, G, G * NBP)).reshape(here * G, G * NBP)
    keep = iota((here * G, G * NBP), 0) % G == iota((here * G, G * NBP), 1) // PER % G
    mixer = jnp.where(keep, spun, 0.0).astype(jnp.bfloat16)

    def differ(i, carry):
        pair = [
            basis[pl.ds(pl.multiple_of((2 * i + j) * (G * NBP), G * NBP), G * NBP), :] for j in range(2)
        ]
        model = dot(mixer, jnp.concatenate(pair, axis=1))
        for j in range(2):
            top = pl.multiple_of((2 * i + j) * G, G)
            spot = pl.ds(pl.multiple_of(top + SHIFT, SHIFT), G)
            for e in range(here):
                fitted = model[e * G : (e + 1) * G, j * W : (j + 1) * W]
                diff = science[e, pl.ds(top, G), :].astype(jnp.float32) - fitted
                mass = lives[e] * weights[e, pl.ds(top, G), :]
                moved[e, spot, :] = pltpu.roll(mass * diff, runs[e], 1)
        return carry

    lax.fori_loop(0, H // G // 2, differ, 0)

    prod_sides = gather_sky(1)
    mass_done()
    total = total_of(0)
    prod_sides()
    prod_done = merge(1)
    root = lax.rsqrt(1.0 + total)
    prod_done()
    coadd_out[...] = total_of(1) * root


def local(mesh_sizes, template, science, weights, shifts, valid, counts):
    tiles, epochs = mesh_sizes
    rows = template.shape[1]
    here = science.shape[1]
    field = pltpu.VMEM((2, epochs, rows, W), jnp.float32)
    tile = pltpu.VMEM((H, W), jnp.float32)
    cols = column_taps()
    bands = row_taps()
    coadd, coefs = pl.pallas_call(
        functools.partial(kernel, tiles, epochs),
        out_shape=(
            jax.ShapeDtypeStruct((rows, W), jnp.float32),
            jax.ShapeDtypeStruct((here, NB), jnp.float32),
        ),
        in_specs=[VMEM, HBM, HBM, SMEM, SMEM, SMEM, HBM, HBM],
        out_specs=(VMEM, VMEM),
        scratch_shapes=[
            pltpu.VMEM((here, H, W), jnp.bfloat16),
            pltpu.VMEM((here, H, W), jnp.float32),
            pltpu.VMEM(cols.shape, jnp.float32),
            pltpu.VMEM(bands.shape, jnp.float32),
            pltpu.VMEM(cols.shape, jnp.bfloat16),
            pltpu.VMEM(cols.shape, jnp.bfloat16),
            pltpu.VMEM(bands.shape, jnp.bfloat16),
            pltpu.VMEM(bands.shape, jnp.bfloat16),
            tile,
            tile,
            tile,
            pltpu.VMEM((NF, H + 2 * G, W), jnp.bfloat16),
            pltpu.VMEM((NF, H + 2 * G, W), jnp.bfloat16),
            pltpu.VMEM((H * NBP, W), jnp.bfloat16),
            pltpu.VMEM((here * NBP, G * W), jnp.bfloat16),
            pltpu.VMEM((NBP + SCI, G * W), jnp.bfloat16),
            pltpu.VMEM((here * NBP, NBP + SCI), jnp.float32),
            pltpu.VMEM((here, H + 2 * SHIFT, W), jnp.float32),
            field,
            field,
            field,
            field,
            field,
            pltpu.SemaphoreType.DMA((4,)),
            pltpu.SemaphoreType.DMA((3, epochs)),
            pltpu.SemaphoreType.DMA((3, epochs)),
            pltpu.SemaphoreType.DMA((3, 2)),
            pltpu.SemaphoreType.DMA((3, 2)),
        ],
        compiler_params=pltpu.CompilerParams(
            collective_id=0, has_side_effects=True, vmem_limit_bytes=60 * 1024 * 1024
        ),
        name="difference_coadd",
    )(template[0], science[0], weights[0], shifts, valid, counts, cols, bands)
    return (coadd[None], coefs[None])


def solution(mesh):
    sizes = (mesh.shape["tile"], mesh.shape["epoch"])
    in_specs = (
        P("tile", "epoch", None),
        P("tile", "epoch", None, None),
        P("tile", "epoch", None, None),
        P("epoch", None),
        P("tile", "epoch"),
        P("tile"),
    )
    out_specs = (P("tile", "epoch", None), P("tile", "epoch", None))
    return jax.shard_map(
        functools.partial(local, sizes), mesh=mesh, in_specs=in_specs, out_specs=out_specs, check_vma=False
    )
```

```python
import functools

import jax
import jax.numpy as jnp
import numpy as np
from jax import lax
from jax.experimental import pallas as pl
from jax.experimental.pallas import tpu as pltpu
from jax.sharding import PartitionSpec as P

NB = 45
PER = 16
HALF = 11
SHIFT = 8
W = 128
H = 256
G = 16
WIN = 3 * G
SIGMAS = (0.75, 1.5, 3.0)
NF = 15
NS = 3
NBP = NS * PER
RIDGE = 0.5
SCI = 16
MESH = pl.DeviceIdType.MESH
VMEM = pl.BlockSpec(memory_space=pltpu.VMEM)
SMEM = pl.BlockSpec(memory_space=pltpu.SMEM)
HBM = pl.BlockSpec(memory_space=pltpu.HBM)


def taps(offset, sigma, power):
    ratio = offset.astype(np.float64) / sigma
    values = ratio**power * np.exp(-0.5 * ratio * ratio)
    return np.where(np.abs(offset) <= HALF, values, 0.0)


def column_taps():
    spot = np.arange(W)
    source = np.concatenate([spot, np.where(spot < W // 2, spot + W, spot - W)])
    offset = spot[None, :] - source[:, None]
    return np.concatenate([taps(offset, s, p) for s in SIGMAS for p in range(5)], axis=1).astype(np.float32)


def row_taps():
    offset = np.arange(G)[:, None] + G - np.arange(WIN)[None, :]
    out = np.zeros((NS, G, PER, 5, WIN))
    for i, sigma in enumerate(SIGMAS):
        for b, (p, q) in enumerate((p, q) for p in range(5) for q in range(5 - p)):
            out[i, :, b, p, :] = taps(offset, sigma, q)
    return out.reshape(NS, G * PER, 5 * WIN).astype(np.float32)


def greet(tiles, epochs, tile, me):
    barrier = pltpu.get_barrier_semaphore()

    def hello(step, carry):
        peer = lax.rem(me + step, epochs)
        pl.semaphore_signal(barrier, inc=1, device_id=(tile, peer), device_id_type=MESH)
        return carry

    lax.fori_loop(1, epochs, hello, 0)
    for step in (1, tiles - 1):
        near = lax.rem(tile + step, tiles)
        pl.semaphore_signal(barrier, inc=1, device_id=(near, me), device_id_type=MESH)

def dot(a, b):
    return jnp.dot(a, b, preferred_element_type=jnp.float32)


def halves(values):
    high = values.astype(jnp.bfloat16)
    return high, (values - high.astype(jnp.float32)).astype(jnp.bfloat16)


def iota(shape, axis):
    return lax.broadcasted_iota(jnp.int32, shape, axis)


def kernel(
    tiles, epochs,
    template, science_hbm, weights_hbm, shifts, valid, counts, col_hbm, row_hbm,
    numer_out, total_out, coef_out,
    science, weights, col_wide, row_wide, ch, cl, rh, rl,
    own, left, right, fh, fl, basis, lhs0, rhs0, lhs1, rhs1, gram, moved, whole, spill, from_left, from_right, parts,
    load, send, recv, side_send, side_recv,
):
    tile = lax.axis_index("tile")
    me = lax.axis_index("epoch")
    here = science.shape[0]
    bands, rows = whole.shape[1], whole.shape[2]
    lane = iota((H, W), 1)
    has_left = (tile > 0).astype(jnp.float32)
    has_right = (tile < tiles - 1).astype(jnp.float32)

    loads = [
        pltpu.make_async_copy(src, dst, load.at[i])
        for i, (src, dst) in enumerate(
            ((weights_hbm, weights), (col_hbm, col_wide), (row_hbm, row_wide), (science_hbm, science))
        )
    ]
    for one in loads:
        one.start()
    greet(tiles, epochs, tile, me)
    moved[:, 0:SHIFT, :] = jnp.zeros((here, SHIFT, W), jnp.float32)
    moved[:, SHIFT + H :, :] = jnp.zeros((here, SHIFT, W), jnp.float32)
    zeros = jnp.zeros((NF, G, W), jnp.bfloat16)
    for buf in (fh, fl):
        buf[:, 0:G, :] = zeros
        buf[:, G + H : G + H + G, :] = zeros
    gram[...] = jnp.zeros_like(gram)
    lhs1[...] = jnp.zeros_like(lhs1)
    rhs1[...] = jnp.zeros_like(rhs1)
    pl.semaphore_wait(pltpu.get_barrier_semaphore(), epochs + 1)

    def to_peers(kind, source, target):
        def copy(step):
            return pltpu.make_async_remote_copy(
                src_ref=source(lax.rem(me + step, epochs)),
                dst_ref=target(step),
                send_sem=send.at[kind, step],
                recv_sem=recv.at[kind, step],
                device_id=(tile, lax.rem(me + step, epochs)),
                device_id_type=MESH,
            )

        def start(step, carry):
            copy(step).start()
            return carry

        def finish(step, carry):
            copy(step).wait_recv()
            copy(step).wait_send()
            return carry

        lax.fori_loop(1, epochs, start, 0)
        return lambda: lax.fori_loop(1, epochs, finish, 0)

    def to_sides(kind, source, to_right, to_left):
        sides = [
            pltpu.make_async_remote_copy(
                src_ref=source,
                dst_ref=target,
                send_sem=side_send.at[kind, i],
                recv_sem=side_recv.at[kind, i],
                device_id=(lax.rem(tile + step, tiles), me),
                device_id_type=MESH,
            )
            for i, (step, target) in enumerate(((1, to_right), (tiles - 1, to_left)))
        ]
        for side in sides:
            side.start()

        def finish():
            for side in sides:
                side.wait()

        return finish

    band = pl.ds(pl.multiple_of(me * rows, rows), rows)
    template_done = to_peers(0, lambda peer: template, lambda step: own.at[band])
    own[band, :] = template[...]

    lives = [
        (valid[0, e] * (me * here + e < counts[0]).astype(jnp.int32)).astype(jnp.float32)
        for e in range(here)
    ]
    runs = [lax.rem(shifts[1, e] + W, W) for e in range(here)]

    def gather_sky(field):
        sky = jnp.zeros((H, W), jnp.float32)
        over = jnp.zeros((H, W), jnp.float32)
        for e in range(here):
            values = moved[e, pl.ds(SHIFT - shifts[0, e], H), :]
            origin = lane - shifts[1, e]
            inside = (origin >= 0) & (origin < W)
            sky += jnp.where(inside, values, 0.0)
            over += jnp.where(inside, 0.0, values)
        whole[field] = sky.reshape(bands, rows, W)
        spill[field] = over.reshape(bands, rows, W)
        return to_sides(1 + field, spill.at[field], from_left.at[field], from_right.at[field])

    def merge(field):
        spot = iota((bands, rows, W), 2)
        whole[field] = whole[field] + (
            jnp.where(spot < SHIFT, from_left[field], 0.0) * has_left
            + jnp.where(spot >= W - SHIFT, from_right[field], 0.0) * has_right
        )
        return to_peers(
            1 + field, lambda peer: whole.at[field, peer], lambda step: parts.at[field, step]
        )

    def total_of(field):
        def add(step, total):
            return total + parts[field, step]

        return lax.fori_loop(1, epochs, add, whole[field, me])

    loads[0].wait()
    for e in range(here):
        moved[e, SHIFT : SHIFT + H, :] = pltpu.roll(lives[e] * weights[e], runs[e], 1)
    loads[1].wait()
    ch[...], cl[...] = halves(col_wide[...])
    loads[2].wait()
    rh[...], rl[...] = halves(row_wide[...])

    template_done()
    tile_sides = to_sides(0, own, left, right)
    mass_sides = gather_sky(0)
    tile_sides()

    mean = 1.0 / (H * W)
    mid = own[...] - jnp.sum(own[...]) * mean
    before = (left[...] - jnp.sum(left[...]) * mean) * has_left
    after = (right[...] - jnp.sum(right[...]) * mean) * has_right
    high, low = halves(jnp.concatenate([mid, jnp.where(lane < W // 2, after, before)], axis=1))
    for f in range(NF):
        cols = slice(f * W, (f + 1) * W)
        out = dot(high, ch[:, cols]) + (dot(low, ch[:, cols]) + dot(high, cl[:, cols]))
        fhigh, flow = halves(out)
        fh[f, G : G + H, :] = fhigh
        fl[f, G : G + H, :] = flow

    mass_sides()
    mass_done = merge(0)
    loads[3].wait()
    turn_to = iota((G * SCI, here * G), 0)
    turn_from = iota((G * SCI, here * G), 1)
    turn = (
        (turn_to // SCI == turn_from % G) & (turn_to % SCI == turn_from // G)
    ).astype(jnp.float32).astype(jnp.bfloat16)

    def make(i, lhs, rhs):
        top = pl.multiple_of(i * G, G)
        pieces = []
        for s in range(NS):
            wh = fh[5 * s : 5 * s + 5, pl.ds(top, WIN), :].reshape(5 * WIN, W)
            wl = fl[5 * s : 5 * s + 5, pl.ds(top, WIN), :].reshape(5 * WIN, W)
            both = dot(rh[s], jnp.concatenate([wh, wl], axis=1))
            values = both[:, :W] + (both[:, W:] + dot(rl[s], wh))
            pieces.append(values.astype(jnp.bfloat16))
            first = pl.multiple_of(i * (G * NBP) + s * (G * PER), G * PER)
            basis[pl.ds(first, G * PER), :] = pieces[s]
        images = science[:, pl.ds(top, G), :].reshape(here * G, W)
        turned = dot(turn, images).astype(jnp.bfloat16)
        for r in range(G):
            cols = slice(r * W, (r + 1) * W)
            part = jnp.concatenate([piece[r * PER : (r + 1) * PER, :] for piece in pieces], axis=0)
            rhs[0:NBP, cols] = part
            rhs[NBP : NBP + SCI, cols] = turned[r * SCI : (r + 1) * SCI, :]
            wide = part.astype(jnp.float32)
            for e in range(here):
                lhs[e * NBP : (e + 1) * NBP, cols] = (
                    wide * weights[e, pl.ds(top + r, 1), :]
                ).astype(jnp.bfloat16)

    def accumulate(lhs, rhs):
        gram[...] += lax.dot_general(
            lhs[...], rhs[...], (((1,), (1,)), ((), ())), preferred_element_type=jnp.float32
        )

    def blocks(i, carry):
        accumulate(lhs1, rhs1)
        make(2 * i, lhs0, rhs0)
        accumulate(lhs0, rhs0)
        make(2 * i + 1, lhs1, rhs1)
        return carry

    lax.fori_loop(0, H // G // 2, blocks, 0)
    accumulate(lhs1, rhs1)

    eye = (iota((NBP, NBP), 0) == iota((NBP, NBP), 1)).astype(jnp.float32)
    col = iota((NBP, SCI), 1)
    systems = []
    scales = []
    for e in range(here):
        full = gram[e * NBP : (e + 1) * NBP, :]
        square = full[:, :NBP]
        square = 0.5 * (square + square.T)
        diag = square * eye
        down = lax.rsqrt(jnp.sum(diag, axis=1, keepdims=True) + 1e-06)
        across = lax.rsqrt(jnp.sum(diag, axis=0, keepdims=True) + 1e-06)
        proj = jnp.sum(jnp.where(col == e, full[:, NBP:], 0.0), axis=1, keepdims=True) * down
        square = square * (down * across) + RIDGE * eye
        systems.append(jnp.concatenate([square, jnp.where(col == 0, proj, 0.0)], axis=1))
        scales.append(across)
    rows_of = iota((NBP, 1), 0)
    for k in [k for k in range(NBP) if k % PER != PER - 1]:
        unit = (rows_of == k).astype(jnp.float32)
        for e in range(here):
            a = systems[e]
            pivot = a[k : k + 1, :]
            pivot = pivot * (1.0 / a[k : k + 1, k : k + 1])
            systems[e] = a - (a[:, k : k + 1] - unit) * pivot
    ys = [jnp.sum(systems[e][:, NBP : NBP + 1] * eye, axis=0, keepdims=True) for e in range(here)]
    coefs = jnp.concatenate([lives[e] * ys[e] for e in range(here)], axis=0)
    coef_out[...] = coefs
    ks = jnp.concatenate([ys[e] * scales[e] for e in range(here)], axis=0).astype(jnp.bfloat16)
    lanes = iota((NBP, G * NBP), 1)
    spread = (lanes // (G * PER) * PER + lanes % PER == iota((NBP, G * NBP), 0)).astype(jnp.float32).astype(jnp.bfloat16)
    spun = dot(ks, spread)
    spun = jnp.broadcast_to(spun[:, None, :], (here, G, G * NBP)).reshape(here * G, G * NBP)
    keep = iota((here * G, G * NBP), 0) % G == iota((here * G, G * NBP), 1) // PER % G
    mixer = jnp.where(keep, spun, 0.0).astype(jnp.bfloat16)

    def differ(i, carry):
        pair = [
            basis[pl.ds(pl.multiple_of((2 * i + j) * (G * NBP), G * NBP), G * NBP), :] for j in range(2)
        ]
        model = dot(mixer, jnp.concatenate(pair, axis=1))
        for j in range(2):
            top = pl.multiple_of((2 * i + j) * G, G)
            spot = pl.ds(pl.multiple_of(top + SHIFT, SHIFT), G)
            for e in range(here):
                fitted = model[e * G : (e + 1) * G, j * W : (j + 1) * W]
                diff = science[e, pl.ds(top, G), :].astype(jnp.float32) - fitted
                mass = lives[e] * weights[e, pl.ds(top, G), :]
                moved[e, spot, :] = pltpu.roll(mass * diff, runs[e], 1)
        return carry

    lax.fori_loop(0, H // G // 2, differ, 0)

    prod_sides = gather_sky(1)
    mass_done()
    total = total_of(0)
    prod_sides()
    prod_done = merge(1)
    total_out[...] = total
    prod_done()
    numer_out[...] = total_of(1)


def finish_kernel(numer, total, coefs, coadd_out, coef_out):
    coadd_out[...] = numer[...] * lax.rsqrt(1.0 + total[...])
    coef_out[...] = jnp.concatenate(
        [coefs[:, s * PER : (s + 1) * PER - 1] for s in range(NS)], axis=1
    )


def local(mesh_sizes, template, science, weights, shifts, valid, counts):
    tiles, epochs = mesh_sizes
    rows = template.shape[1]
    here = science.shape[1]
    field = pltpu.VMEM((2, epochs, rows, W), jnp.float32)
    tile = pltpu.VMEM((H, W), jnp.float32)
    cols = column_taps()
    bands = row_taps()
    coadd_type = jax.ShapeDtypeStruct((rows, W), jnp.float32)
    sums = pl.pallas_call(
        functools.partial(kernel, tiles, epochs),
        out_shape=(coadd_type, coadd_type, jax.ShapeDtypeStruct((here, NBP), jnp.float32)),
        in_specs=[VMEM, HBM, HBM, SMEM, SMEM, SMEM, HBM, HBM],
        out_specs=(VMEM, VMEM, VMEM),
        scratch_shapes=[
            pltpu.VMEM((here, H, W), jnp.bfloat16),
            pltpu.VMEM((here, H, W), jnp.float32),
            pltpu.VMEM(cols.shape, jnp.float32),
            pltpu.VMEM(bands.shape, jnp.float32),
            pltpu.VMEM(cols.shape, jnp.bfloat16),
            pltpu.VMEM(cols.shape, jnp.bfloat16),
            pltpu.VMEM(bands.shape, jnp.bfloat16),
            pltpu.VMEM(bands.shape, jnp.bfloat16),
            tile,
            tile,
            tile,
            pltpu.VMEM((NF, H + 2 * G, W), jnp.bfloat16),
            pltpu.VMEM((NF, H + 2 * G, W), jnp.bfloat16),
            pltpu.VMEM((H * NBP, W), jnp.bfloat16),
            pltpu.VMEM((here * NBP, G * W), jnp.bfloat16),
            pltpu.VMEM((NBP + SCI, G * W), jnp.bfloat16),
            pltpu.VMEM((here * NBP, G * W), jnp.bfloat16),
            pltpu.VMEM((NBP + SCI, G * W), jnp.bfloat16),
            pltpu.VMEM((here * NBP, NBP + SCI), jnp.float32),
            pltpu.VMEM((here, H + 2 * SHIFT, W), jnp.float32),
            field,
            field,
            field,
            field,
            field,
            pltpu.SemaphoreType.DMA((4,)),
            pltpu.SemaphoreType.DMA((3, epochs)),
            pltpu.SemaphoreType.DMA((3, epochs)),
            pltpu.SemaphoreType.DMA((3, 2)),
            pltpu.SemaphoreType.DMA((3, 2)),
        ],
        compiler_params=pltpu.CompilerParams(
            collective_id=0, has_side_effects=True, vmem_limit_bytes=60 * 1024 * 1024
        ),
        name="difference_coadd",
    )(template[0], science[0], weights[0], shifts.T, valid, counts, cols, bands)
    coadd, coefs = pl.pallas_call(
        finish_kernel,
        out_shape=(coadd_type, jax.ShapeDtypeStruct((here, NB), jnp.float32)),
        in_specs=[VMEM] * 3,
        out_specs=(VMEM, VMEM),
        name="finish",
    )(*sums)
    return (coadd[None], coefs[None])


def solution(mesh):
    sizes = (mesh.shape["tile"], mesh.shape["epoch"])
    in_specs = (
        P("tile", "epoch", None),
        P("tile", "epoch", None, None),
        P("tile", "epoch", None, None),
        P("epoch", None),
        P("tile", "epoch"),
        P("tile"),
    )
    out_specs = (P("tile", "epoch", None), P("tile", "epoch", None))
    return jax.shard_map(
        functools.partial(local, sizes), mesh=mesh, in_specs=in_specs, out_specs=out_specs, check_vma=False
    )
```

```python
import functools

import jax
import jax.numpy as jnp
import numpy as np
from jax import lax
from jax.experimental import pallas as pl
from jax.experimental.pallas import tpu as pltpu
from jax.sharding import PartitionSpec as P

NB = 45
PER = 16
HALF = 11
SHIFT = 8
W = 128
H = 256
G = 16
WIN = 3 * G
SIGMAS = (0.75, 1.5, 3.0)
NF = 15
NS = 3
NBP = NS * PER
RIDGE = 0.5
SCI = 16
MESH = pl.DeviceIdType.MESH
VMEM = pl.BlockSpec(memory_space=pltpu.VMEM)
SMEM = pl.BlockSpec(memory_space=pltpu.SMEM)
HBM = pl.BlockSpec(memory_space=pltpu.HBM)


def taps(offset, sigma, power):
    ratio = offset.astype(np.float64) / sigma
    values = ratio**power * np.exp(-0.5 * ratio * ratio)
    return np.where(np.abs(offset) <= HALF, values, 0.0)


def column_taps():
    spot = np.arange(W)
    source = np.concatenate([spot, np.where(spot < W // 2, spot + W, spot - W)])
    offset = spot[None, :] - source[:, None]
    return np.concatenate([taps(offset, s, p) for s in SIGMAS for p in range(5)], axis=1).astype(np.float32)


def row_taps():
    offset = np.arange(G)[:, None] + G - np.arange(WIN)[None, :]
    out = np.zeros((NS, G, PER, 5, WIN))
    for i, sigma in enumerate(SIGMAS):
        for b, (p, q) in enumerate((p, q) for p in range(5) for q in range(5 - p)):
            out[i, :, b, p, :] = taps(offset, sigma, q)
    return out.reshape(NS, G * PER, 5 * WIN).astype(np.float32)


def greet(tiles, epochs, tile, me):
    barrier = pltpu.get_barrier_semaphore()

    def hello(step, carry):
        peer = lax.rem(me + step, epochs)
        pl.semaphore_signal(barrier, inc=1, device_id=(tile, peer), device_id_type=MESH)
        return carry

    lax.fori_loop(1, epochs, hello, 0)
    for step in (1, tiles - 1):
        near = lax.rem(tile + step, tiles)
        pl.semaphore_signal(barrier, inc=1, device_id=(near, me), device_id_type=MESH)

def dot(a, b):
    return jnp.dot(a, b, preferred_element_type=jnp.float32)


def halves(values):
    high = values.astype(jnp.bfloat16)
    return high, (values - high.astype(jnp.float32)).astype(jnp.bfloat16)


def iota(shape, axis):
    return lax.broadcasted_iota(jnp.int32, shape, axis)


def kernel(
    tiles, epochs,
    template, science_hbm, weights_hbm, shifts, valid, counts, col_hbm, row_hbm,
    numer_out, total_out, coef_out,
    science, weights, col_wide, row_wide, ch, cl, rh, rl,
    own, left, right, fh, fl, basis, lhs0, rhs0, lhs1, rhs1, gram, moved, whole, spill, from_left, from_right, parts,
    load, send, recv, side_send, side_recv,
):
    tile = lax.axis_index("tile")
    me = lax.axis_index("epoch")
    here = science.shape[0]
    bands, rows = whole.shape[1], whole.shape[2]
    lane = iota((H, W), 1)
    has_left = (tile > 0).astype(jnp.float32)
    has_right = (tile < tiles - 1).astype(jnp.float32)

    loads = [
        pltpu.make_async_copy(src, dst, load.at[i])
        for i, (src, dst) in enumerate(
            ((weights_hbm, weights), (col_hbm, col_wide), (row_hbm, row_wide), (science_hbm, science))
        )
    ]
    for one in loads:
        one.start()
    greet(tiles, epochs, tile, me)
    moved[:, 0:SHIFT, :] = jnp.zeros((here, SHIFT, W), jnp.float32)
    moved[:, SHIFT + H :, :] = jnp.zeros((here, SHIFT, W), jnp.float32)
    zeros = jnp.zeros((NF, G, W), jnp.bfloat16)
    for buf in (fh, fl):
        buf[:, 0:G, :] = zeros
        buf[:, G + H : G + H + G, :] = zeros
    gram[...] = jnp.zeros_like(gram)
    lhs1[...] = jnp.zeros_like(lhs1)
    rhs1[...] = jnp.zeros_like(rhs1)
    pl.semaphore_wait(pltpu.get_barrier_semaphore(), epochs + 1)

    def to_peers(kind, source, target):
        def copy(step):
            return pltpu.make_async_remote_copy(
                src_ref=source(lax.rem(me + step, epochs)),
                dst_ref=target(step),
                send_sem=send.at[kind, step],
                recv_sem=recv.at[kind, step],
                device_id=(tile, lax.rem(me + step, epochs)),
                device_id_type=MESH,
            )

        def start(step, carry):
            copy(step).start()
            return carry

        def finish(step, carry):
            copy(step).wait_recv()
            copy(step).wait_send()
            return carry

        lax.fori_loop(1, epochs, start, 0)
        return lambda: lax.fori_loop(1, epochs, finish, 0)

    def to_sides(kind, source, to_right, to_left):
        sides = [
            pltpu.make_async_remote_copy(
                src_ref=source,
                dst_ref=target,
                send_sem=side_send.at[kind, i],
                recv_sem=side_recv.at[kind, i],
                device_id=(lax.rem(tile + step, tiles), me),
                device_id_type=MESH,
            )
            for i, (step, target) in enumerate(((1, to_right), (tiles - 1, to_left)))
        ]
        for side in sides:
            side.start()

        def finish():
            for side in sides:
                side.wait()

        return finish

    band = pl.ds(pl.multiple_of(me * rows, rows), rows)
    template_done = to_peers(0, lambda peer: template, lambda step: own.at[band])
    own[band, :] = template[...]

    lives = [
        (valid[0, e] * (me * here + e < counts[0]).astype(jnp.int32)).astype(jnp.float32)
        for e in range(here)
    ]
    runs = [lax.rem(shifts[1, e] + W, W) for e in range(here)]

    def gather_sky(field):
        over = jnp.zeros((H, W), jnp.float32)
        for e in range(here):
            origin = lane - shifts[1, e]
            outside = (origin < 0) | (origin >= W)
            over += jnp.where(outside, moved[e, pl.ds(SHIFT - shifts[0, e], H), :], 0.0)
        spill[field] = over.reshape(bands, rows, W)
        sides = to_sides(1 + field, spill.at[field], from_left.at[field], from_right.at[field])
        sky = jnp.zeros((H, W), jnp.float32)
        for e in range(here):
            origin = lane - shifts[1, e]
            inside = (origin >= 0) & (origin < W)
            sky += jnp.where(inside, moved[e, pl.ds(SHIFT - shifts[0, e], H), :], 0.0)
        whole[field] = sky.reshape(bands, rows, W)
        return sides

    def merge(field):
        spot = iota((bands, rows, W), 2)
        whole[field] = whole[field] + (
            jnp.where(spot < SHIFT, from_left[field], 0.0) * has_left
            + jnp.where(spot >= W - SHIFT, from_right[field], 0.0) * has_right
        )
        return to_peers(
            1 + field, lambda peer: whole.at[field, peer], lambda step: parts.at[field, step]
        )

    def total_of(field):
        def add(step, total):
            return total + parts[field, step]

        return lax.fori_loop(1, epochs, add, whole[field, me])

    loads[0].wait()
    for e in range(here):
        moved[e, SHIFT : SHIFT + H, :] = pltpu.roll(lives[e] * weights[e], runs[e], 1)
    loads[1].wait()
    ch[...], cl[...] = halves(col_wide[...])
    loads[2].wait()
    rh[...], rl[...] = halves(row_wide[...])

    template_done()
    tile_sides = to_sides(0, own, left, right)
    mass_sides = gather_sky(0)
    tile_sides()

    mean = 1.0 / (H * W)
    mid = own[...] - jnp.sum(own[...]) * mean
    before = (left[...] - jnp.sum(left[...]) * mean) * has_left
    after = (right[...] - jnp.sum(right[...]) * mean) * has_right
    high, low = halves(jnp.concatenate([mid, jnp.where(lane < W // 2, after, before)], axis=1))
    for f in range(NF):
        cols = slice(f * W, (f + 1) * W)
        out = dot(high, ch[:, cols]) + (dot(low, ch[:, cols]) + dot(high, cl[:, cols]))
        fhigh, flow = halves(out)
        fh[f, G : G + H, :] = fhigh
        fl[f, G : G + H, :] = flow

    mass_sides()
    mass_done = merge(0)
    loads[3].wait()
    turn_to = iota((G * SCI, here * G), 0)
    turn_from = iota((G * SCI, here * G), 1)
    turn = (
        (turn_to // SCI == turn_from % G) & (turn_to % SCI == turn_from // G)
    ).astype(jnp.float32).astype(jnp.bfloat16)

    def make(i, lhs, rhs):
        top = pl.multiple_of(i * G, G)
        pieces = []
        for s in range(NS):
            wh = fh[5 * s : 5 * s + 5, pl.ds(top, WIN), :].reshape(5 * WIN, W)
            wl = fl[5 * s : 5 * s + 5, pl.ds(top, WIN), :].reshape(5 * WIN, W)
            both = dot(rh[s], jnp.concatenate([wh, wl], axis=1))
            values = both[:, :W] + (both[:, W:] + dot(rl[s], wh))
            pieces.append(values.astype(jnp.bfloat16))
            first = pl.multiple_of(i * (G * NBP) + s * (G * PER), G * PER)
            basis[pl.ds(first, G * PER), :] = pieces[s]
        images = science[:, pl.ds(top, G), :].reshape(here * G, W)
        turned = dot(turn, images).astype(jnp.bfloat16)
        for r in range(G):
            cols = slice(r * W, (r + 1) * W)
            part = jnp.concatenate([piece[r * PER : (r + 1) * PER, :] for piece in pieces], axis=0)
            rhs[0:NBP, cols] = part
            rhs[NBP : NBP + SCI, cols] = turned[r * SCI : (r + 1) * SCI, :]
            wide = part.astype(jnp.float32)
            for e in range(here):
                lhs[e * NBP : (e + 1) * NBP, cols] = (
                    wide * weights[e, pl.ds(top + r, 1), :]
                ).astype(jnp.bfloat16)

    def accumulate(lhs, rhs):
        gram[...] += lax.dot_general(
            lhs[...], rhs[...], (((1,), (1,)), ((), ())), preferred_element_type=jnp.float32
        )

    def blocks(i, carry):
        accumulate(lhs1, rhs1)
        make(2 * i, lhs0, rhs0)
        accumulate(lhs0, rhs0)
        make(2 * i + 1, lhs1, rhs1)
        return carry

    lax.fori_loop(0, H // G // 2, blocks, 0)
    accumulate(lhs1, rhs1)

    eye = (iota((NBP, NBP), 0) == iota((NBP, NBP), 1)).astype(jnp.float32)
    col = iota((NBP, SCI), 1)
    systems = []
    scales = []
    for e in range(here):
        full = gram[e * NBP : (e + 1) * NBP, :]
        square = full[:, :NBP]
        square = 0.5 * (square + square.T)
        diag = square * eye
        down = lax.rsqrt(jnp.sum(diag, axis=1, keepdims=True) + 1e-06)
        across = lax.rsqrt(jnp.sum(diag, axis=0, keepdims=True) + 1e-06)
        proj = jnp.sum(jnp.where(col == e, full[:, NBP:], 0.0), axis=1, keepdims=True) * down
        square = square * (down * across) + RIDGE * eye
        systems.append(jnp.concatenate([square, jnp.where(col == 0, proj, 0.0)], axis=1))
        scales.append(across)
    rows_of = iota((NBP, 1), 0)
    for k in [k for k in range(NBP) if k % PER != PER - 1]:
        unit = (rows_of == k).astype(jnp.float32)
        for e in range(here):
            a = systems[e]
            pivot = a[k : k + 1, :]
            pivot = pivot * (1.0 / a[k : k + 1, k : k + 1])
            systems[e] = a - (a[:, k : k + 1] - unit) * pivot
    ys = [jnp.sum(systems[e][:, NBP : NBP + 1] * eye, axis=0, keepdims=True) for e in range(here)]
    coefs = jnp.concatenate([lives[e] * ys[e] for e in range(here)], axis=0)
    coef_out[...] = coefs
    ks = jnp.concatenate([ys[e] * scales[e] for e in range(here)], axis=0).astype(jnp.bfloat16)
    lanes = iota((NBP, G * NBP), 1)
    spread = (lanes // (G * PER) * PER + lanes % PER == iota((NBP, G * NBP), 0)).astype(jnp.float32).astype(jnp.bfloat16)
    spun = dot(ks, spread)
    spun = jnp.broadcast_to(spun[:, None, :], (here, G, G * NBP)).reshape(here * G, G * NBP)
    keep = iota((here * G, G * NBP), 0) % G == iota((here * G, G * NBP), 1) // PER % G
    mixer = jnp.where(keep, spun, 0.0).astype(jnp.bfloat16)

    def differ(i, carry):
        pair = [
            basis[pl.ds(pl.multiple_of((2 * i + j) * (G * NBP), G * NBP), G * NBP), :] for j in range(2)
        ]
        model = dot(mixer, jnp.concatenate(pair, axis=1))
        for j in range(2):
            top = pl.multiple_of((2 * i + j) * G, G)
            spot = pl.ds(pl.multiple_of(top + SHIFT, SHIFT), G)
            for e in range(here):
                fitted = model[e * G : (e + 1) * G, j * W : (j + 1) * W]
                diff = science[e, pl.ds(top, G), :].astype(jnp.float32) - fitted
                mass = lives[e] * weights[e, pl.ds(top, G), :]
                moved[e, spot, :] = pltpu.roll(mass * diff, runs[e], 1)
        return carry

    lax.fori_loop(0, H // G // 2, differ, 0, unroll=4)

    prod_sides = gather_sky(1)
    mass_done()
    total = total_of(0)
    prod_sides()
    prod_done = merge(1)
    total_out[...] = total
    prod_done()
    numer_out[...] = total_of(1)


def finish_kernel(numer, total, coefs, coadd_out, coef_out):
    coadd_out[...] = numer[...] * lax.rsqrt(1.0 + total[...])
    coef_out[...] = jnp.concatenate(
        [coefs[:, s * PER : (s + 1) * PER - 1] for s in range(NS)], axis=1
    )


def local(mesh_sizes, template, science, weights, shifts, valid, counts):
    tiles, epochs = mesh_sizes
    rows = template.shape[1]
    here = science.shape[1]
    field = pltpu.VMEM((2, epochs, rows, W), jnp.float32)
    tile = pltpu.VMEM((H, W), jnp.float32)
    cols = column_taps()
    bands = row_taps()
    coadd_type = jax.ShapeDtypeStruct((rows, W), jnp.float32)
    sums = pl.pallas_call(
        functools.partial(kernel, tiles, epochs),
        out_shape=(coadd_type, coadd_type, jax.ShapeDtypeStruct((here, NBP), jnp.float32)),
        in_specs=[VMEM, HBM, HBM, SMEM, SMEM, SMEM, HBM, HBM],
        out_specs=(VMEM, VMEM, VMEM),
        scratch_shapes=[
            pltpu.VMEM((here, H, W), jnp.bfloat16),
            pltpu.VMEM((here, H, W), jnp.float32),
            pltpu.VMEM(cols.shape, jnp.float32),
            pltpu.VMEM(bands.shape, jnp.float32),
            pltpu.VMEM(cols.shape, jnp.bfloat16),
            pltpu.VMEM(cols.shape, jnp.bfloat16),
            pltpu.VMEM(bands.shape, jnp.bfloat16),
            pltpu.VMEM(bands.shape, jnp.bfloat16),
            tile,
            tile,
            tile,
            pltpu.VMEM((NF, H + 2 * G, W), jnp.bfloat16),
            pltpu.VMEM((NF, H + 2 * G, W), jnp.bfloat16),
            pltpu.VMEM((H * NBP, W), jnp.bfloat16),
            pltpu.VMEM((here * NBP, G * W), jnp.bfloat16),
            pltpu.VMEM((NBP + SCI, G * W), jnp.bfloat16),
            pltpu.VMEM((here * NBP, G * W), jnp.bfloat16),
            pltpu.VMEM((NBP + SCI, G * W), jnp.bfloat16),
            pltpu.VMEM((here * NBP, NBP + SCI), jnp.float32),
            pltpu.VMEM((here, H + 2 * SHIFT, W), jnp.float32),
            field,
            field,
            field,
            field,
            field,
            pltpu.SemaphoreType.DMA((4,)),
            pltpu.SemaphoreType.DMA((3, epochs)),
            pltpu.SemaphoreType.DMA((3, epochs)),
            pltpu.SemaphoreType.DMA((3, 2)),
            pltpu.SemaphoreType.DMA((3, 2)),
        ],
        compiler_params=pltpu.CompilerParams(
            collective_id=0, has_side_effects=True, vmem_limit_bytes=60 * 1024 * 1024
        ),
        name="difference_coadd",
    )(template[0], science[0], weights[0], shifts.T, valid, counts, cols, bands)
    coadd, coefs = pl.pallas_call(
        finish_kernel,
        out_shape=(coadd_type, jax.ShapeDtypeStruct((here, NB), jnp.float32)),
        in_specs=[VMEM] * 3,
        out_specs=(VMEM, VMEM),
        name="finish",
    )(*sums)
    return (coadd[None], coefs[None])


def solution(mesh):
    sizes = (mesh.shape["tile"], mesh.shape["epoch"])
    in_specs = (
        P("tile", "epoch", None),
        P("tile", "epoch", None, None),
        P("tile", "epoch", None, None),
        P("epoch", None),
        P("tile", "epoch"),
        P("tile"),
    )
    out_specs = (P("tile", "epoch", None), P("tile", "epoch", None))
    return jax.shard_map(
        functools.partial(local, sizes), mesh=mesh, in_specs=in_specs, out_specs=out_specs, check_vma=False
    )
```
